1024 devices in a mesh: dp: 8 (over y), expert: 16 (over z), tensor: 8 (over x, core).
Axes of the slice: x: 4, y: 8, z: 16, core: 2. Of those that a mesh axis runs over, the one named last changes fastest.
Arguments:
- activations: bfloat16 [16384, 4096], P(('dp', 'expert'), 'tensor'), parts along dimension 0, may hold values from -6 to 6
- expert_ids: int32 [16384, 8], P(('dp', 'expert')), parts along dimension 0, may hold values from 0 to 31, all different within a row; in each aligned block of 128 rows (0 to 127, 128 to 255, ...) at most 48 rows name the same one
- route_gates: float32 [16384, 8], P(('dp', 'expert')), parts along dimension 0, may hold values from 0.1 to 1
- down_proj: bfloat16 [4096, 1024], P('tensor'), may hold values from -0.09375 to 0.09375
- expert_gate: bfloat16 [32, 1024, 2688], P('expert', None, 'tensor'), may hold values from -0.1875 to 0.1875
- expert_up: bfloat16 [32, 1024, 2688], P('expert', None, 'tensor'), may hold values from -0.1875 to 0.1875
- expert_down: bfloat16 [32, 2688, 1024], P('expert', 'tensor'), may hold values from -0.125 to 0.125
- up_proj: bfloat16 [1024, 4096], P(None, 'tensor'), may hold values from -0.1875 to 0.1875
Outputs:
- layer_out: bfloat16 [16384, 4096], P(('dp', 'expert'), 'tensor'), parts along dimension 0
The draws below stay inside these ranges and needn't reach their ends.
There are 8 independent parts, one for each index of `dp`. The reference program is written for one: setup_inputs(seed, part) draws one part's arguments, and reference() takes and returns one part's arrays. A program takes and returns all parts, laid end to end along the dimension named above; an argument that names none is the same for every part. Nothing has to cross between parts.
Inputs may be any that keep to these rules, and one draw needn't show every extreme that they name: `expert_ids`: each row names 8 different experts; within the rows of one block of 128 tokens no expert is named more than 48 times, a bound that some block reaches.
All inputs are finite; a program needn't handle non-finite values.
Results may differ from the reference program's by a relative error of at most 0.035.
Values may be sent and summed in bfloat16 or wider, within the bound.
No kernel may reach another device: no remote copies, remote signals or barrier semaphores. Data moves between devices by JAX's collectives and lax.ppermute only.
A program may use at most 64 MiB of HBM per device.

```python
import math
import jax
import jax.numpy as jnp
import numpy as np
from jax import lax

D = 4096
L = 1024
FF = 2688
TOPK = 8
TOK_DEV = 128
EXPERTS = 32
TOKENS = 2048
CAP = 48
N_EXPERT = 16
N_TENSOR = 8


def steps_of(own_key, extent, cuts, smallest, top_value):
    level = 1.0
    for dim, shards_of in cuts:
        steps = jax.random.uniform(jax.random.fold_in(jax.random.fold_in(own_key, 6), dim), (shards_of,), jnp.float32, smallest / len(cuts), top_value / len(cuts))
        level = level * jnp.repeat(jnp.exp(steps), extent[dim] // shards_of).reshape((-1,) + (1,) * (len(extent) - 1 - dim))
    return level


def routed_block(rng, own, number, rows, number_of, top, reach, lean):
    ranking = jax.random.permutation(rng, number_of)
    heavy_load, common = load_shares(number_of, rows * top, reach, lean, True), load_shares(number_of, rows * top, reach, lean, False)
    places = jnp.arange(number_of)

    def named(lengths, rotation):
        used = int((lengths > 0).sum())
        fixed = max(1, used // 4)
        moved = fixed + (places - fixed + rotation * (used - fixed)) % max(1, number_of - fixed)
        return jnp.zeros((number_of,), jnp.int32).at[ranking[jnp.where(places < fixed, places, moved)]].set(jnp.asarray(lengths, jnp.int32))

    lengths = jnp.where(number % 4 == 0, named(heavy_load, number // 4), named(common, number - number // 4 - 1))
    mixed = jax.random.permutation(jax.random.fold_in(own, 3), number_of)
    source_of, sink = mixed[0:number_of // 2 * 2:2], mixed[1:number_of // 2 * 2:2]
    room = jnp.minimum(lengths[source_of] - 1, reach - lengths[sink]) // 2
    room = jnp.where((source_of == ranking[0]) | (sink == ranking[0]) | (lengths[sink] == 0), 0, jnp.maximum(room, 0))
    moved = jax.random.randint(jax.random.fold_in(own, 4), (number_of // 2,), 0, 1 << 20) % (room + 1)
    lengths = lengths.at[source_of].add(-moved).at[sink].add(moved)
    labels = jnp.searchsorted(jnp.cumsum(lengths), jnp.arange(rows * top), side="right").astype(jnp.int32)
    grid = labels.reshape(top, rows).T
    grid = grid[jax.random.permutation(jax.random.fold_in(own, 1), rows)]
    rotation = jax.random.randint(jax.random.fold_in(own, 2), (rows, 1), 0, top)
    return jnp.take_along_axis(grid, (jnp.arange(top)[None, :] + rotation) % top, axis=1)


def load_shares(amount, total, most, slope, full):
    weights = [(1 << 20) // math.isqrt(rank ** slope) + 1 for rank in range(1, amount + 1)]
    largest = most if full else min(most, max(-(-total // amount), total * weights[0] // sum(weights)))
    least = 1 if total - largest >= amount - 1 else 0
    given, rest = [largest] + [least] * (amount - 1), total - largest - least * (amount - 1)
    while rest > 0:
        movable = [i for i in range(1, amount) if given[i] < largest] or [i for i in range(1, amount) if given[i] < most]
        whole, budget = sum([weights[i] for i in movable]), rest
        for i in movable:
            extra = min(most - given[i], max(1, budget * weights[i] // whole), rest)
            given[i] = given[i] + extra
            rest = rest - extra
    return np.array(given)


def gaussian(stream_key, extent, width, reach, shards=(), kind=jnp.bfloat16):
    loudness = steps_of(stream_key, extent, shards, -0.22, 0.18) if shards else 1.0
    array = jax.random.normal(stream_key, extent, jnp.float32) * width * loudness
    return jnp.minimum(jnp.maximum(array, -reach), reach).astype(kind)


def setup_inputs(seed: int = 0, part: int = 0) -> dict:
    streams_of = jax.random.split(jax.random.key(seed), 9)
    own_keys = jax.random.split(jax.random.fold_in(streams_of[8], part), 9)
    activations = gaussian(own_keys[0], (TOKENS, D), 1.0, 6.0, ((0, 16), (1, 8)))
    expert_ids_keys = jax.random.split(jax.random.fold_in(own_keys[1], 1), TOKENS // TOK_DEV)
    expert_ids_turns = jax.random.permutation(jax.random.fold_in(own_keys[1], 3), TOKENS // TOK_DEV)
    expert_ids = jax.vmap(lambda own, number: routed_block(jax.random.fold_in(own_keys[1], 2), own, number, TOK_DEV, EXPERTS, TOPK, CAP, 2))(expert_ids_keys, expert_ids_turns).reshape((TOKENS, TOPK))
    route_gates = jnp.clip(jnp.exp(math.log(1.0) - 2.3025851 * jax.random.uniform(own_keys[2], (TOKENS, TOPK), jnp.float32) ** steps_of(own_keys[2], (TOKENS, TOPK), ((0, 16),), -0.2, 0.2)), 0.1, 1.0)
    down_proj = gaussian(streams_of[3], (D, L), D ** -0.5, 0.09375, ((0, 8),))
    expert_gate = gaussian(streams_of[4], (EXPERTS, L, FF), L ** -0.5, 0.1875, ((0, 16), (2, 8)))
    expert_up = gaussian(streams_of[5], (EXPERTS, L, FF), L ** -0.5, 0.1875, ((0, 16), (2, 8)))
    expert_down = gaussian(streams_of[6], (EXPERTS, FF, L), FF ** -0.5, 0.125, ((0, 16), (1, 8)))
    up_proj = gaussian(streams_of[7], (L, D), L ** -0.5, 0.1875, ((1, 8),))
    return dict(activations=activations, expert_ids=expert_ids, route_gates=route_gates, down_proj=down_proj, expert_gate=expert_gate, expert_up=expert_up, expert_down=expert_down, up_proj=up_proj)


def expert_block(args):
    rows, gate_w, up_w, down_w = args
    gate = jnp.dot(rows, gate_w, preferred_element_type=jnp.float32)
    upper = jnp.dot(rows, up_w, preferred_element_type=jnp.float32)
    hidden = (jax.nn.silu(gate) * upper).astype(jnp.bfloat16)
    group = FF // N_TENSOR
    hidden_g = hidden.reshape(hidden.shape[0], N_TENSOR, group).astype(jnp.float32)
    down_g = down_w.reshape(N_TENSOR, group, L).astype(jnp.float32)
    parts = jnp.einsum("rgf,gfl->grl", hidden_g, down_g)
    parts = parts.astype(jnp.bfloat16).astype(jnp.float32)
    return jnp.sum(parts, axis=0).astype(jnp.bfloat16)


def reference(activations, expert_ids, route_gates, down_proj, expert_gate, expert_up, expert_down, up_proj):
    latent = jnp.dot(activations, down_proj, preferred_element_type=jnp.float32).astype(jnp.bfloat16)
    blocks = expert_ids.reshape(N_EXPERT, TOK_DEV * TOPK)
    onehot = (blocks[:, :, None] == jnp.arange(EXPERTS, dtype=jnp.int32)[None, None, :]).astype(jnp.int32)
    before = jnp.cumsum(onehot, axis=1) - onehot
    slot = jnp.sum(before * onehot, axis=-1).astype(jnp.int32)
    source = jnp.arange(N_EXPERT, dtype=jnp.int32)[:, None]
    dest = (blocks * (N_EXPERT * CAP) + source * CAP + slot).reshape(-1).astype(jnp.int32)
    count = TOKENS * TOPK
    owner = jnp.zeros((EXPERTS * N_EXPERT * CAP,), jnp.int32).at[dest].set(jnp.arange(count, dtype=jnp.int32) + 1)
    filled = owner > 0
    token_idx = jnp.maximum(owner - 1, 0) // TOPK
    rows = jnp.where(filled[:, None], latent[token_idx], jnp.zeros((), jnp.bfloat16))
    rows = rows.reshape(EXPERTS, N_EXPERT * CAP, L)
    outs = lax.map(expert_block, (rows, expert_gate, expert_up, expert_down))
    values = outs.reshape(-1, L)[dest].reshape(TOKENS, TOPK, L).astype(jnp.float32)
    combined = jnp.sum(route_gates[:, :, None] * values, axis=1).astype(jnp.bfloat16)
    return jnp.dot(combined, up_proj, preferred_element_type=jnp.float32).astype(jnp.bfloat16)
```

```python
import jax
import jax.numpy as jnp
from jax import lax
from jax.experimental import pallas as pl
from jax.experimental.pallas import tpu as pltpu
from jax.sharding import Mesh, PartitionSpec as P

F32 = jnp.float32
BF16 = jnp.bfloat16
CAP = 48


def iota(shape, dim):
    return lax.broadcasted_iota(jnp.int32, shape, dim)


def dot(a, b):
    return jnp.dot(a, b, preferred_element_type=F32)


def routes(core, ids_ref, gates_ref, experts, rows):
    ids = ids_ref[...]
    tokens, top = ids.shape
    named = 2 * iota((tokens, experts), 1) + core
    mask = jnp.zeros((tokens, experts), F32)
    gate = jnp.zeros((tokens, experts), F32)
    for k in range(top):
        same = (ids[:, k : k + 1] == named).astype(F32)
        mask += same
        if gates_ref is not None:
            gate += gates_ref[:, k : k + 1] * same
    earlier = (iota((tokens, tokens), 0) > iota((tokens, tokens), 1)).astype(BF16)
    slot = dot(earlier, mask.astype(BF16))
    code = (mask * (slot + 1.0) - 1.0).astype(BF16)
    first = iota((experts, rows), 0) * CAP
    column = iota((experts, rows), 1)
    spread = ((column >= first) & (column < first + CAP)).astype(BF16)
    place = lax.rem(iota((tokens, rows), 1), CAP).astype(F32)
    hit = (dot(code, spread) == place).astype(F32)
    if gates_ref is None:
        return hit.astype(BF16), None, None
    high = gate.astype(BF16)
    low = (gate - high.astype(F32)).astype(BF16)
    return None, (hit * dot(high, spread)).astype(BF16), (hit * dot(low, spread)).astype(BF16)


def dispatch_kernel(core_ref, ids_ref, own_ref, other_ref, out_ref):
    latent = (own_ref[...] + other_ref[...]).astype(BF16)
    hit, _, _ = routes(core_ref[0], ids_ref, None, out_ref.shape[0] // CAP, out_ref.shape[0])
    out_ref[...] = lax.dot_general(
        hit, latent, (((0,), (0,)), ((), ())), preferred_element_type=F32
    ).astype(BF16)


def combine_kernel(core_ref, ids_ref, gates_ref, rows_ref, out_ref):
    rows = rows_ref[...]
    _, high, low = routes(core_ref[0], ids_ref, gates_ref, rows.shape[0] // CAP, rows.shape[0])
    out_ref[...] = dot(high, rows) + dot(low, rows)


def ffn_kernel(core_ref, x_ref, gate_ref, up_ref, down_ref, gate2_ref, up2_ref, down2_ref, out_ref, wide, deep):
    units = gate_ref.shape[2]
    pitch = deep.shape[0] // 2

    @pl.when(pl.program_id(0) == 0)
    def _():
        for i, ref in enumerate((gate_ref, gate2_ref, up_ref, up2_ref)):
            value = ref[0] if len(ref.shape) == 3 else ref[...]
            wide[:, i * pitch : i * pitch + units] = value
            wide[:, i * pitch + units : (i + 1) * pitch] = jnp.zeros((wide.shape[0], pitch - units), BF16)
        for i, ref in enumerate((down_ref, down2_ref)):
            value = ref[0] if len(ref.shape) == 3 else ref[...]
            deep[i * pitch : i * pitch + units, :] = value
            deep[i * pitch + units : (i + 1) * pitch, :] = jnp.zeros((pitch - units, deep.shape[1]), BF16)

    parts, _, width = x_ref.shape
    x = jnp.concatenate([x_ref[i] for i in range(parts)], axis=1)
    both = dot(x, wide[...])
    gate, up = both[:, : 2 * pitch], both[:, 2 * pitch :]
    hidden = (gate / (1.0 + jnp.exp(-gate)) * up).astype(BF16)
    result = dot(hidden, deep[...]).astype(BF16)
    for i in range(parts):
        out_ref[i] = result[:, i * width : (i + 1) * width]


def ffn(core, x, gate, up, down, gate2, up2, down2):
    parts, rows, width = x.shape
    _, latent, units = gate.shape
    pitch = -(-units // 128) * 128
    block = 256
    mine = lambda shape: pl.BlockSpec((1,) + shape, lambda i, c: (c[0], 0, 0))
    whole = lambda shape: pl.BlockSpec(shape, lambda i, c: (0, 0))
    return pl.pallas_call(
        ffn_kernel,
        out_shape=jax.ShapeDtypeStruct((parts, rows, width), BF16),
        grid_spec=pltpu.PrefetchScalarGridSpec(
            num_scalar_prefetch=1,
            grid=(rows // block,),
            in_specs=[
                pl.BlockSpec((parts, block, width), lambda i, c: (0, i, 0)),
                mine((latent, units)),
                mine((latent, units)),
                mine((units, latent)),
                whole((latent, units)),
                whole((latent, units)),
                whole((units, latent)),
            ],
            out_specs=pl.BlockSpec((parts, block, width), lambda i, c: (0, i, 0)),
            scratch_shapes=[pltpu.VMEM((latent, 4 * pitch), BF16), pltpu.VMEM((2 * pitch, latent), BF16)],
        ),
        compiler_params=pltpu.CompilerParams(vmem_limit_bytes=48 << 20),
    )(core, x, gate, up, down, gate2, up2, down2)


def body(activations, expert_ids, route_gates, down_proj, expert_gate, expert_up, expert_down, up_proj):
    chips = lax.axis_size("x")
    owners = lax.axis_size("z")
    core = lax.axis_index("c").astype(jnp.int32)
    tokens = activations.shape[0]
    latent = down_proj.shape[1]
    width = latent // chips
    rows = owners * CAP
    swap = lambda a: lax.ppermute(a, "c", [(0, 1), (1, 0)])
    other = lambda w: swap(lax.dynamic_index_in_dim(w, 1 - core, 0, keepdims=False))
    here = pl.BlockSpec(memory_space=pltpu.VMEM)
    scalar = pl.BlockSpec(memory_space=pltpu.SMEM)
    index = core.reshape(1)

    gate2, up2, down2 = other(expert_gate), other(expert_up), other(expert_down)
    partial = jnp.concatenate(
        [dot(activations, down_proj[:, i * width : (i + 1) * width]).astype(BF16)[None] for i in range(chips)]
    )
    share = jnp.sum(lax.all_to_all(partial, "x", 0, 0, tiled=True).astype(F32), axis=0)
    sent = pl.pallas_call(
        dispatch_kernel,
        out_shape=jax.ShapeDtypeStruct((rows, width), BF16),
        in_specs=[scalar, here, here, here],
        out_specs=here,
    )(index, expert_ids, share, swap(share))
    got = lax.all_to_all(sent.reshape(owners, CAP, width), "z", 0, 0, tiled=True).reshape(rows, width)
    full = lax.all_gather(got, "x", axis=0)
    terms = ffn(index, full, expert_gate, expert_up, expert_down, gate2, up2, down2)
    summed = lax.psum_scatter(terms, "x", scatter_dimension=0, tiled=False)
    back = lax.all_to_all(summed.reshape(owners, CAP, width), "z", 0, 0, tiled=True).reshape(rows, width)
    mine = pl.pallas_call(
        combine_kernel,
        out_shape=jax.ShapeDtypeStruct((tokens, width), F32),
        in_specs=[scalar, here, here, here],
        out_specs=here,
    )(index, expert_ids, route_gates, back)
    combined = (mine + swap(mine)).astype(BF16)
    parts = lax.all_to_all(jnp.broadcast_to(combined[None], (chips, tokens, width)), "x", 0, 0, tiled=True)
    result = sum(dot(parts[i], up_proj[i * width : (i + 1) * width]) for i in range(chips))
    return result.astype(BF16)


def solution(mesh):
    shape = mesh.devices.shape
    split = Mesh(mesh.devices.reshape(shape[0], shape[1], shape[2] // 2, 2), ("dp", "z", "x", "c"))
    tensor = ("x", "c")
    in_specs = (
        P(("dp", "z"), tensor),
        P(("dp", "z"), None),
        P(("dp", "z"), None),
        P(tensor, None),
        P("z", None, tensor),
        P("z", None, tensor),
        P("z", tensor, None),
        P(None, tensor),
    )
    return jax.shard_map(body, mesh=split, in_specs=in_specs, out_specs=P(("dp", "z"), tensor), check_vma=False)
```

```python
import jax
import jax.numpy as jnp
from jax import lax
from jax.experimental import pallas as pl
from jax.experimental.pallas import tpu as pltpu
from jax.sharding import Mesh, PartitionSpec as P

F32 = jnp.float32
BF16 = jnp.bfloat16
CAP = 48


def iota(shape, dim):
    return lax.broadcasted_iota(jnp.int32, shape, dim)


def dot(a, b):
    return jnp.dot(a, b, preferred_element_type=F32)


def dot_dims(a, b, i, j):
    return lax.dot_general(a, b, (((i,), (j,)), ((), ())), preferred_element_type=F32)


def routes_kernel(core_ref, ids_ref, gates_ref, hit_ref, weight_ref):
    ids, gates = ids_ref[...], gates_ref[...]
    top, tokens = ids.shape
    rows = hit_ref.shape[0]
    experts = rows // CAP
    named = 2 * iota((experts, tokens), 0) + core_ref[0]
    mask = jnp.zeros((experts, tokens), F32)
    gate = jnp.zeros((experts, tokens), F32)
    for k in range(top):
        same = (ids[k : k + 1, :] == named).astype(F32)
        mask += same
        gate += gates[k : k + 1, :] * same
    earlier = (iota((tokens, tokens), 0) < iota((tokens, tokens), 1)).astype(BF16)
    slot = dot(mask.astype(BF16), earlier)
    code = (mask * (slot + 1.0) - 1.0).astype(BF16)
    first = iota((rows, experts), 1) * CAP
    row = iota((rows, experts), 0)
    spread = ((row >= first) & (row < first + CAP)).astype(BF16)
    place = lax.rem(iota((rows, tokens), 0), CAP).astype(F32)
    hit = dot(spread, code) == place
    hit_ref[...] = jnp.where(hit, 1.0, 0.0).astype(BF16)
    high = gate.astype(BF16)
    low = (gate - high.astype(F32)).astype(BF16)
    for i, term in enumerate((high, low)):
        weight_ref[i * tokens : (i + 1) * tokens, :] = jnp.where(hit, dot(spread, term), 0.0).T.astype(BF16)


def latent_kernel(a_ref, w_ref, out_ref):
    result = dot(a_ref[...], w_ref[...]).astype(BF16)
    parts, _, width = out_ref.shape
    for i in range(parts):
        first = i // 2 * width
        out_ref[i] = result[:, first : first + width]


def dispatch_kernel(hit_ref, pieces_ref, out_ref):
    latent = sum(pieces_ref[i].astype(F32) for i in range(pieces_ref.shape[0])).astype(BF16)
    out_ref[...] = dot(hit_ref[...], latent).astype(BF16)


def combine_kernel(weight_ref, rows_ref, out_ref):
    both = dot(weight_ref[...], rows_ref[...])
    copies, tokens, _ = out_ref.shape
    result = (both[:tokens] + both[tokens:]).astype(BF16)
    for i in range(copies):
        out_ref[i] = result


def ffn_kernel(x_ref, wide_ref, deep_ref, out_ref):
    parts, _, width = x_ref.shape
    units = deep_ref.shape[0]
    x = jnp.concatenate([x_ref[i] for i in range(parts)], axis=1)
    both = dot_dims(x, wide_ref[...], 1, 1)
    gate, up = both[:, :units], both[:, both.shape[1] - units :]
    hidden = (gate / (1.0 + jnp.exp(-gate)) * up).astype(BF16)
    result = dot(hidden, deep_ref[...]).astype(BF16)
    for i in range(parts):
        out_ref[i] = result[:, i * width : (i + 1) * width]


HERE = pl.BlockSpec(memory_space=pltpu.VMEM)
SCALAR = pl.BlockSpec(memory_space=pltpu.SMEM)


def call(kernel, out, *operands):
    specs = [SCALAR if a.shape == (1,) else HERE for a in operands]
    return pl.pallas_call(kernel, out_shape=out, in_specs=specs, out_specs=jax.tree.map(lambda _: HERE, out))(*operands)


def ffn(x, wide, deep):
    parts, rows, width = x.shape
    block = 256
    spec = pl.BlockSpec((parts, block, width), lambda i: (0, i, 0))
    return pl.pallas_call(
        ffn_kernel,
        out_shape=jax.ShapeDtypeStruct((parts, rows, width), BF16),
        grid=(rows // block,),
        in_specs=[spec, HERE, HERE],
        out_specs=spec,
        compiler_params=pltpu.CompilerParams(vmem_limit_bytes=40 << 20),
    )(x, wide, deep)


def body(activations, expert_ids, route_gates, down_proj, expert_gate, expert_up, expert_down, up_proj):
    chips = lax.axis_size("x")
    owners = lax.axis_size("z")
    core = lax.axis_index("c").astype(jnp.int32)
    index = core.reshape(1)
    tokens = activations.shape[0]
    latent = down_proj.shape[1]
    width = latent // chips
    rows = owners * CAP
    ids, gates = expert_ids.T, route_gates.T
    swap = lambda a: lax.ppermute(a, "c", [(0, 1), (1, 0)])
    pick = lambda w, i: lax.dynamic_index_in_dim(w, i, 0, keepdims=False)
    around = lambda a, axis: lax.all_to_all(a, axis, 0, 0, tiled=True)

    shape = lambda dtype, *sizes: jax.ShapeDtypeStruct(sizes, dtype)
    hit, weight = call(routes_kernel, (shape(BF16, rows, tokens), shape(BF16, 2 * tokens, rows)), index, ids, gates)
    partial = call(latent_kernel, shape(BF16, 2 * chips, tokens, width), activations, down_proj)

    weights = (jnp.swapaxes(expert_gate, 1, 2), jnp.swapaxes(expert_up, 1, 2), expert_down)
    partial, weights = lax.optimization_barrier((partial, weights))
    units = expert_down.shape[1]
    leaving = jnp.concatenate([pick(w, 1 - core) for w in weights])
    pieces = around(partial, ("x", "c"))
    pieces, leaving, hit, weight = lax.optimization_barrier((pieces, leaving, hit, weight))
    got = swap(leaving)
    sent = call(dispatch_kernel, shape(BF16, rows, width), hit, pieces)
    pad = jnp.zeros((-2 * units % 128, latent), BF16)
    gate_own, up_own, down_own = [pick(w, core) for w in weights]
    wide = jnp.concatenate([gate_own, got[:units], pad, up_own, got[units : 2 * units]])
    deep = jnp.concatenate([down_own, got[2 * units :]])

    held = around(sent.reshape(owners, CAP, width), "z").reshape(rows, width)
    held, wide, deep = lax.optimization_barrier((held, wide, deep))
    full = around(jnp.broadcast_to(held[None], (chips, rows, width)), "x")
    terms = around(ffn(full, wide, deep), "x")
    summed = jnp.sum(terms.astype(F32), axis=0).astype(BF16)
    back = around(summed.reshape(owners, CAP, width), "z").reshape(rows, width)
    mine = call(combine_kernel, shape(BF16, 2 * chips, tokens, width), weight, back)
    parts = around(mine, ("x", "c")).reshape(chips, 2, tokens, width)
    parts = (parts[:, 0].astype(F32) + parts[:, 1].astype(F32)).astype(BF16)
    result = sum(dot(parts[i], up_proj[i * width : (i + 1) * width]) for i in range(chips))
    return result.astype(BF16)


def solution(mesh):
    shape = mesh.devices.shape
    split = Mesh(mesh.devices.reshape(shape[0], shape[1], shape[2] // 2, 2), ("dp", "z", "x", "c"))
    tensor = ("x", "c")
    in_specs = (
        P(("dp", "z"), tensor),
        P(("dp", "z"), None),
        P(("dp", "z"), None),
        P(tensor, None),
        P("z", None, tensor),
        P("z", None, tensor),
        P("z", tensor, None),
        P(None, tensor),
    )
    return jax.shard_map(body, mesh=split, in_specs=in_specs, out_specs=P(("dp", "z"), tensor), check_vma=False)
```

```python
import jax
import jax.numpy as jnp
from jax import lax
from jax.experimental import pallas as pl
from jax.experimental.pallas import tpu as pltpu
from jax.sharding import Mesh, PartitionSpec as P

F32 = jnp.float32
BF16 = jnp.bfloat16
CAP = 48


def iota(shape, dim):
    return lax.broadcasted_iota(jnp.int32, shape, dim)


def dot(a, b):
    return jnp.dot(a, b, preferred_element_type=F32)


def dot_dims(a, b, i, j):
    return lax.dot_general(a, b, (((i,), (j,)), ((), ())), preferred_element_type=F32)


def routes_kernel(core_ref, ids_ref, gates_ref, hit_ref, weight_ref):
    ids, gates = ids_ref[...], gates_ref[...]
    top, tokens = ids.shape
    rows = hit_ref.shape[0]
    experts = rows // CAP
    named = 2 * iota((experts, tokens), 0) + core_ref[0]
    mask = jnp.zeros((experts, tokens), F32)
    gate = jnp.zeros((experts, tokens), F32)
    for k in range(top):
        same = (ids[k : k + 1, :] == named).astype(F32)
        mask += same
        gate += gates[k : k + 1, :] * same
    earlier = (iota((tokens, tokens), 0) < iota((tokens, tokens), 1)).astype(BF16)
    slot = dot(mask.astype(BF16), earlier)
    code = (mask * (slot + 1.0) - 1.0).astype(BF16)
    first = iota((rows, experts), 1) * CAP
    row = iota((rows, experts), 0)
    spread = ((row >= first) & (row < first + CAP)).astype(BF16)
    place = lax.rem(iota((rows, tokens), 0), CAP).astype(F32)
    hit = dot(spread, code) == place
    hit_ref[...] = jnp.where(hit, 1.0, 0.0).astype(BF16)
    high = gate.astype(BF16)
    low = (gate - high.astype(F32)).astype(BF16)
    for i, term in enumerate((high, low)):
        weight_ref[i * tokens : (i + 1) * tokens, :] = jnp.where(hit, dot(spread, term), 0.0).T.astype(BF16)


def latent_kernel(a_ref, w_ref, out_ref):
    result = dot(a_ref[...], w_ref[...]).astype(BF16)
    parts, _, width = out_ref.shape
    for i in range(parts):
        first = i // 2 * width
        out_ref[i] = result[:, first : first + width]


def dispatch_kernel(hit_ref, pieces_ref, out_ref):
    latent = sum(pieces_ref[i].astype(F32) for i in range(pieces_ref.shape[0])).astype(BF16)
    out_ref[...] = dot(hit_ref[...], latent).astype(BF16)


def combine_kernel(weight_ref, rows_ref, out_ref):
    both = dot(weight_ref[...], rows_ref[...])
    copies, tokens, _ = out_ref.shape
    result = (both[:tokens] + both[tokens:]).astype(BF16)
    for i in range(copies):
        out_ref[i] = result


def output_kernel(own_ref, other_ref, w_ref, out_ref):
    parts = [(own_ref[i].astype(F32) + other_ref[i].astype(F32)).astype(BF16) for i in range(own_ref.shape[0])]
    out_ref[...] = dot(jnp.concatenate(parts, axis=1), w_ref[...]).astype(BF16)


def ffn_kernel(x_ref, wide_ref, deep_ref, out_ref):
    parts, rows, width = x_ref.shape
    units = deep_ref.shape[0]
    block = 256
    for first in range(0, rows, block):
        here = pl.ds(first, block)
        x = jnp.concatenate([x_ref[i, here] for i in range(parts)], axis=1)
        gate = dot_dims(x, wide_ref[:units], 1, 1)
        up = dot_dims(x, wide_ref[wide_ref.shape[0] - units :], 1, 1)
        hidden = (gate / (1.0 + jnp.exp(-gate)) * up).astype(BF16)
        result = dot(hidden, deep_ref[...]).astype(BF16)
        for i in range(parts):
            out_ref[i, here] = result[:, i * width : (i + 1) * width]


HERE = pl.BlockSpec(memory_space=pltpu.VMEM)
SCALAR = pl.BlockSpec(memory_space=pltpu.SMEM)


def call(kernel, out, *operands, limit=8 << 20):
    specs = [SCALAR if a.shape == (1,) else HERE for a in operands]
    return pl.pallas_call(
        kernel,
        out_shape=out,
        in_specs=specs,
        out_specs=jax.tree.map(lambda _: HERE, out),
        compiler_params=pltpu.CompilerParams(vmem_limit_bytes=limit),
    )(*operands)


def body(activations, expert_ids, route_gates, down_proj, expert_gate, expert_up, expert_down, up_proj):
    chips = lax.axis_size("x")
    owners = lax.axis_size("z")
    core = lax.axis_index("c").astype(jnp.int32)
    index = core.reshape(1)
    tokens = activations.shape[0]
    latent = down_proj.shape[1]
    width = latent // chips
    rows = owners * CAP
    ids, gates = expert_ids.T, route_gates.T
    swap = lambda a: lax.ppermute(a, "c", [(0, 1), (1, 0)])
    pick = lambda w, i: lax.dynamic_index_in_dim(w, i, 0, keepdims=False)
    around = lambda a, axis: lax.all_to_all(a, axis, 0, 0, tiled=True)

    shape = lambda dtype, *sizes: jax.ShapeDtypeStruct(sizes, dtype)
    hit, weight = call(routes_kernel, (shape(BF16, rows, tokens), shape(BF16, 2 * tokens, rows)), index, ids, gates)
    partial = call(latent_kernel, shape(BF16, 2 * chips, tokens, width), activations, down_proj, limit=None)

    weights = (jnp.swapaxes(expert_gate, 1, 2), jnp.swapaxes(expert_up, 1, 2), expert_down)
    partial, weights = lax.optimization_barrier((partial, weights))
    units = expert_down.shape[1]
    leaving = jnp.concatenate([pick(w, 1 - core) for w in weights])
    pieces = around(partial, ("x", "c"))
    pieces, leaving, hit, weight = lax.optimization_barrier((pieces, leaving, hit, weight))
    got = swap(leaving)
    sent = call(dispatch_kernel, shape(BF16, rows, width), hit, pieces)
    pad = jnp.zeros((-2 * units % 128, latent), BF16)
    gate_own, up_own, down_own = [pick(w, core) for w in weights]
    wide = jnp.concatenate([gate_own, got[:units], pad, up_own, got[units : 2 * units]])
    deep = jnp.concatenate([down_own, got[2 * units :]])

    held = around(sent.reshape(owners, CAP, width), "z").reshape(rows, width)
    held, wide, deep = lax.optimization_barrier((held, wide, deep))
    full = around(jnp.broadcast_to(held[None], (chips, rows, width)), "x")
    terms = around(call(ffn_kernel, shape(BF16, chips, rows, width), full, wide, deep, limit=24 << 20), "x")
    summed = jnp.sum(terms.astype(F32), axis=0).astype(BF16)
    back = around(summed.reshape(owners, CAP, width), "z").reshape(rows, width)
    mine = call(combine_kernel, shape(BF16, chips, tokens, width), weight, back)
    parts = around(mine, "x")
    return call(output_kernel, shape(BF16, tokens, up_proj.shape[1]), parts, swap(parts), up_proj)


def solution(mesh):
    shape = mesh.devices.shape
    split = Mesh(mesh.devices.reshape(shape[0], shape[1], shape[2] // 2, 2), ("dp", "z", "x", "c"))
    tensor = ("x", "c")
    in_specs = (
        P(("dp", "z"), tensor),
        P(("dp", "z"), None),
        P(("dp", "z"), None),
        P(tensor, None),
        P("z", None, tensor),
        P("z", None, tensor),
        P("z", tensor, None),
        P(None, tensor),
    )
    return jax.shard_map(body, mesh=split, in_specs=in_specs, out_specs=P(("dp", "z"), tensor), check_vma=False)
```

```python
import functools

import jax
import jax.numpy as jnp
from jax import lax
from jax.experimental import pallas as pl
from jax.experimental.pallas import tpu as pltpu
from jax.sharding import Mesh, PartitionSpec as P

F32 = jnp.float32
BF16 = jnp.bfloat16
CAP = 48


def iota(shape, dim):
    return lax.broadcasted_iota(jnp.int32, shape, dim)


def dot(a, b):
    return jnp.dot(a, b, preferred_element_type=F32)


def dot_dims(a, b, i, j):
    return lax.dot_general(a, b, (((i,), (j,)), ((), ())), preferred_element_type=F32)


def routes_kernel(core_ref, ids_ref, gates_ref, hit_ref, weight_ref):
    ids, gates = ids_ref[...], gates_ref[...]
    top, tokens = ids.shape
    rows = hit_ref.shape[0]
    experts = rows // CAP
    named = 2 * iota((experts, tokens), 0) + core_ref[0]
    mask = jnp.zeros((experts, tokens), F32)
    gate = jnp.zeros((experts, tokens), F32)
    for k in range(top):
        same = (ids[k : k + 1, :] == named).astype(F32)
        mask += same
        gate += gates[k : k + 1, :] * same
    earlier = (iota((tokens, tokens), 0) < iota((tokens, tokens), 1)).astype(BF16)
    slot = dot(mask.astype(BF16), earlier)
    code = (mask * (slot + 1.0) - 1.0).astype(BF16)
    first = iota((rows, experts), 1) * CAP
    row = iota((rows, experts), 0)
    spread = ((row >= first) & (row < first + CAP)).astype(BF16)
    place = lax.rem(iota((rows, tokens), 0), CAP).astype(F32)
    hit = dot(spread, code) == place
    hit_ref[...] = jnp.where(hit, 1.0, 0.0).astype(BF16)
    high = gate.astype(BF16)
    low = (gate - high.astype(F32)).astype(BF16)
    for i, term in enumerate((high, low)):
        weight_ref[i * tokens : (i + 1) * tokens, :] = jnp.where(hit, dot(spread, term), 0.0).T.astype(BF16)


def latent_kernel(a_ref, w_ref, out_ref):
    result = dot(a_ref[...], w_ref[...]).astype(BF16)
    parts, _, width = out_ref.shape
    for i in range(parts):
        first = i // 2 * width
        out_ref[i] = result[:, first : first + width]


def dispatch_kernel(hit_ref, pieces_ref, out_ref):
    latent = sum(pieces_ref[i].astype(F32) for i in range(pieces_ref.shape[0])).astype(BF16)
    out_ref[...] = dot(hit_ref[...], latent).astype(BF16)


def combine_kernel(weight_ref, rows_ref, out_ref):
    both = dot(weight_ref[...], rows_ref[...])
    copies, tokens, _ = out_ref.shape
    result = (both[:tokens] + both[tokens:]).astype(BF16)
    for i in range(copies):
        out_ref[i] = result


def output_kernel(own_ref, other_ref, w_ref, out_ref):
    parts = [(own_ref[i].astype(F32) + other_ref[i].astype(F32)).astype(BF16) for i in range(own_ref.shape[0])]
    out_ref[...] = dot(jnp.concatenate(parts, axis=1), w_ref[...]).astype(BF16)


def assemble_kernel(turn, core_ref, gate_ref, up_ref, down_ref, got_ref, out_ref, held_ref, done):
    @pl.when(core_ref[0] == turn)
    def _():
        units = down_ref.shape[1]
        loads, stores = [], []
        for i, ref in enumerate((gate_ref, up_ref, down_ref)):
            halves = (ref.at[core_ref[0]], got_ref.at[pl.ds(i * units, units)])
            for j, half in enumerate(halves):
                n = 2 * i + j
                place = pl.ds(n * units, units)
                loads.append(pltpu.make_async_copy(half, held_ref.at[place], done.at[0, n]))
                stores.append(pltpu.make_async_copy(held_ref.at[place], out_ref.at[place], done.at[1, n]))
        for load in loads:
            load.start()
        for load, store in zip(loads, stores):
            load.wait()
            store.start()
        for store in stores:
            store.wait()


def ffn_kernel(core_ref, x_ref, late_ref, early_ref, out_ref):
    parts, rows, width = x_ref.shape
    block = 256

    def run(w_ref):
        units = w_ref.shape[0] // 3
        for first in range(0, rows, block):
            here = pl.ds(first, block)
            x = jnp.concatenate([x_ref[i, here] for i in range(parts)], axis=1)
            gate = dot_dims(x, w_ref[:units], 1, 1)
            up = dot_dims(x, w_ref[units : 2 * units], 1, 1)
            hidden = (gate / (1.0 + jnp.exp(-gate)) * up).astype(BF16)
            result = dot(hidden, w_ref[2 * units :]).astype(BF16)
            for i in range(parts):
                out_ref[i, here] = result[:, i * width : (i + 1) * width]

    @pl.when(core_ref[0] == 0)
    def _():
        run(late_ref)

    @pl.when(core_ref[0] == 1)
    def _():
        run(early_ref)


HERE = pl.BlockSpec(memory_space=pltpu.VMEM)
FAR = pl.BlockSpec(memory_space=pl.ANY)
SCALAR = pl.BlockSpec(memory_space=pltpu.SMEM)


def call(kernel, out, *operands, limit=8 << 20):
    specs = [SCALAR if a.shape == (1,) else HERE for a in operands]
    return pl.pallas_call(
        kernel,
        out_shape=out,
        in_specs=specs,
        out_specs=jax.tree.map(lambda _: HERE, out),
        compiler_params=pltpu.CompilerParams(vmem_limit_bytes=limit),
    )(*operands)


def body(activations, expert_ids, route_gates, down_proj, expert_gate, expert_up, expert_down, up_proj):
    chips = lax.axis_size("x")
    owners = lax.axis_size("z")
    core = lax.axis_index("c").astype(jnp.int32)
    index = core.reshape(1)
    tokens = activations.shape[0]
    latent = down_proj.shape[1]
    width = latent // chips
    rows = owners * CAP
    ids, gates = expert_ids.T, route_gates.T
    swap = lambda a: lax.ppermute(a, "c", [(0, 1), (1, 0)])
    pick = lambda w, i: lax.dynamic_index_in_dim(w, i, 0, keepdims=False)
    around = lambda a, axis: lax.all_to_all(a, axis, 0, 0, tiled=True)

    shape = lambda dtype, *sizes: jax.ShapeDtypeStruct(sizes, dtype)
    hit, weight = call(routes_kernel, (shape(BF16, rows, tokens), shape(BF16, 2 * tokens, rows)), index, ids, gates)
    partial = call(latent_kernel, shape(BF16, 2 * chips, tokens, width), activations, down_proj, limit=None)

    weights = (jnp.swapaxes(expert_gate, 1, 2), jnp.swapaxes(expert_up, 1, 2), expert_down)
    partial, weights = lax.optimization_barrier((partial, weights))
    units = expert_down.shape[1]
    leaving = jnp.concatenate([pick(w, 1 - core) for w in weights])
    pieces = around(partial, ("x", "c"))
    pieces, leaving, hit, weight = lax.optimization_barrier((pieces, leaving, hit, weight))
    got = swap(leaving)
    sent = call(dispatch_kernel, shape(BF16, rows, width), hit, pieces)

    def assemble(turn, *operands):
        return pl.pallas_call(
            functools.partial(assemble_kernel, turn),
            out_shape=shape(BF16, 6 * units, latent),
            in_specs=[SCALAR] + [FAR] * 4,
            out_specs=FAR,
            scratch_shapes=[pltpu.VMEM((6 * units, latent), BF16), pltpu.SemaphoreType.DMA((2, 6))],
            compiler_params=pltpu.CompilerParams(vmem_limit_bytes=56 << 20),
        )(index, *operands)

    whole = assemble(1, *weights, got)
    held = around(sent.reshape(owners, CAP, width), "z").reshape(rows, width)
    held, whole, weights, got = lax.optimization_barrier((held, whole, weights, got))
    late = assemble(0, *weights, got)
    held, whole, late = lax.optimization_barrier((held, whole, late))
    full = around(jnp.broadcast_to(held[None], (chips, rows, width)), "x")
    out = call(ffn_kernel, shape(BF16, chips, rows, width), index, full, late, whole, limit=12 << 20)
    terms = around(out, "x")
    summed = jnp.sum(terms.astype(F32), axis=0).astype(BF16)
    back = around(summed.reshape(owners, CAP, width), "z").reshape(rows, width)
    mine = call(combine_kernel, shape(BF16, chips, tokens, width), weight, back)
    parts = around(mine, "x")
    return call(output_kernel, shape(BF16, tokens, up_proj.shape[1]), parts, swap(parts), up_proj)


def solution(mesh):
    shape = mesh.devices.shape
    split = Mesh(mesh.devices.reshape(shape[0], shape[1], shape[2] // 2, 2), ("dp", "z", "x", "c"))
    tensor = ("x", "c")
    in_specs = (
        P(("dp", "z"), tensor),
        P(("dp", "z"), None),
        P(("dp", "z"), None),
        P(tensor, None),
        P("z", None, tensor),
        P("z", None, tensor),
        P("z", tensor, None),
        P(None, tensor),
    )
    return jax.shard_map(body, mesh=split, in_specs=in_specs, out_specs=P(("dp", "z"), tensor), check_vma=False)
```

```python
import functools

import jax
import jax.numpy as jnp
from jax import lax
from jax.experimental import pallas as pl
from jax.experimental.pallas import tpu as pltpu
from jax.sharding import Mesh, PartitionSpec as P

F32 = jnp.float32
BF16 = jnp.bfloat16
CAP = 48


def iota(shape, dim):
    return lax.broadcasted_iota(jnp.int32, shape, dim)


def dot(a, b):
    return jnp.dot(a, b, preferred_element_type=F32)


def dot_dims(a, b, i, j):
    return lax.dot_general(a, b, (((i,), (j,)), ((), ())), preferred_element_type=F32)


def routes_kernel(core_ref, ids_ref, gates_ref, hit_ref, weight_ref):
    ids, gates = ids_ref[...], gates_ref[...]
    top, tokens = ids.shape
    rows = hit_ref.shape[0]
    experts = rows // CAP
    named = 2 * iota((experts, tokens), 0) + core_ref[0]
    mask = jnp.zeros((experts, tokens), F32)
    gate = jnp.zeros((experts, tokens), F32)
    for k in range(top):
        same = (ids[k : k + 1, :] == named).astype(F32)
        mask += same
        gate += gates[k : k + 1, :] * same
    earlier = (iota((tokens, tokens), 0) < iota((tokens, tokens), 1)).astype(BF16)
    slot = dot(mask.astype(BF16), earlier)
    code = (mask * (slot + 1.0) - 1.0).astype(BF16)
    first = iota((rows, experts), 1) * CAP
    row = iota((rows, experts), 0)
    spread = ((row >= first) & (row < first + CAP)).astype(BF16)
    place = lax.rem(iota((rows, tokens), 0), CAP).astype(F32)
    hit = dot(spread, code) == place
    hit_ref[...] = jnp.where(hit, 1.0, 0.0).astype(BF16)
    high = gate.astype(BF16)
    low = (gate - high.astype(F32)).astype(BF16)
    for i, term in enumerate((high, low)):
        weight_ref[i * tokens : (i + 1) * tokens, :] = jnp.where(hit, dot(spread, term), 0.0).T.astype(BF16)


def latent_kernel(a_ref, w_ref, out_ref):
    result = dot(a_ref[...], w_ref[...]).astype(BF16)
    parts, _, width = out_ref.shape
    for i in range(parts):
        first = i // 2 * width
        out_ref[i] = result[:, first : first + width]


def dispatch_kernel(hit_ref, pieces_ref, out_ref):
    latent = sum(pieces_ref[i].astype(F32) for i in range(pieces_ref.shape[0])).astype(BF16)
    out_ref[...] = dot(hit_ref[...], latent).astype(BF16)


def combine_kernel(weight_ref, rows_ref, out_ref):
    both = dot(weight_ref[...], rows_ref[...])
    tokens = out_ref.shape[0]
    out_ref[...] = (both[:tokens] + both[tokens:]).astype(BF16)


def merge_kernel(own_ref, other_ref, out_ref):
    result = (own_ref[...].astype(F32) + other_ref[...].astype(F32)).astype(BF16)
    for i in range(out_ref.shape[0]):
        out_ref[i] = result


def output_kernel(x_ref, w_ref, out_ref):
    x = jnp.concatenate([x_ref[i] for i in range(x_ref.shape[0])], axis=1)
    out_ref[...] = dot(x, w_ref[...]).astype(BF16)


def assemble_kernel(turn, core_ref, gate_ref, up_ref, down_ref, got_ref, out_ref, held_ref, done):
    @pl.when(core_ref[0] == turn)
    def _():
        units = down_ref.shape[1]
        loads, stores = [], []
        for i, ref in enumerate((gate_ref, up_ref, down_ref)):
            halves = (ref.at[core_ref[0]], got_ref.at[pl.ds(i * units, units)])
            for j, half in enumerate(halves):
                n = 2 * i + j
                place = pl.ds(n * units, units)
                loads.append(pltpu.make_async_copy(half, held_ref.at[place], done.at[0, n]))
                stores.append(pltpu.make_async_copy(held_ref.at[place], out_ref.at[place], done.at[1, n]))
        for load in loads:
            load.start()
        for load, store in zip(loads, stores):
            load.wait()
            store.start()
        for store in stores:
            store.wait()


def ffn_kernel(core_ref, x_ref, late_ref, early_ref, out_ref):
    parts, rows, width = x_ref.shape
    block = 256

    def run(w_ref):
        units = w_ref.shape[0] // 3
        for first in range(0, rows, block):
            here = pl.ds(first, block)
            x = jnp.concatenate([x_ref[i, here] for i in range(parts)], axis=1)
            gate = dot_dims(x, w_ref[:units], 1, 1)
            up = dot_dims(x, w_ref[units : 2 * units], 1, 1)
            hidden = (gate / (1.0 + jnp.exp(-gate)) * up).astype(BF16)
            result = dot(hidden, w_ref[2 * units :]).astype(BF16)
            for i in range(parts):
                out_ref[i, here] = result[:, i * width : (i + 1) * width]

    @pl.when(core_ref[0] == 0)
    def _():
        run(late_ref)

    @pl.when(core_ref[0] == 1)
    def _():
        run(early_ref)


HERE = pl.BlockSpec(memory_space=pltpu.VMEM)
FAR = pl.BlockSpec(memory_space=pl.ANY)
SCALAR = pl.BlockSpec(memory_space=pltpu.SMEM)


def call(kernel, out, *operands, limit=8 << 20):
    specs = [SCALAR if a.shape == (1,) else HERE for a in operands]
    return pl.pallas_call(
        kernel,
        out_shape=out,
        in_specs=specs,
        out_specs=jax.tree.map(lambda _: HERE, out),
        compiler_params=pltpu.CompilerParams(vmem_limit_bytes=limit),
    )(*operands)


def body(activations, expert_ids, route_gates, down_proj, expert_gate, expert_up, expert_down, up_proj):
    chips = lax.axis_size("x")
    owners = lax.axis_size("z")
    core = lax.axis_index("c").astype(jnp.int32)
    index = core.reshape(1)
    tokens = activations.shape[0]
    latent = down_proj.shape[1]
    width = latent // chips
    rows = owners * CAP
    ids, gates = expert_ids.T, route_gates.T
    swap = lambda a: lax.ppermute(a, "c", [(0, 1), (1, 0)])
    pick = lambda w, i: lax.dynamic_index_in_dim(w, i, 0, keepdims=False)
    around = lambda a, axis: lax.all_to_all(a, axis, 0, 0, tiled=True)

    shape = lambda dtype, *sizes: jax.ShapeDtypeStruct(sizes, dtype)
    hit, weight = call(routes_kernel, (shape(BF16, rows, tokens), shape(BF16, 2 * tokens, rows)), index, ids, gates)
    partial = call(latent_kernel, shape(BF16, 2 * chips, tokens, width), activations, down_proj, limit=None)

    weights = (jnp.swapaxes(expert_gate, 1, 2), jnp.swapaxes(expert_up, 1, 2), expert_down)
    partial, weights = lax.optimization_barrier((partial, weights))
    units = expert_down.shape[1]
    leaving = jnp.concatenate([pick(w, 1 - core) for w in weights])
    pieces = around(partial, ("x", "c"))
    pieces, leaving, hit, weight = lax.optimization_barrier((pieces, leaving, hit, weight))
    got = swap(leaving)
    sent = call(dispatch_kernel, shape(BF16, rows, width), hit, pieces)

    def assemble(turn, *operands):
        return pl.pallas_call(
            functools.partial(assemble_kernel, turn),
            out_shape=shape(BF16, 6 * units, latent),
            in_specs=[SCALAR] + [FAR] * 4,
            out_specs=FAR,
            scratch_shapes=[pltpu.VMEM((6 * units, latent), BF16), pltpu.SemaphoreType.DMA((2, 6))],
            compiler_params=pltpu.CompilerParams(vmem_limit_bytes=56 << 20),
        )(index, *operands)

    whole = assemble(1, *weights, got)
    held = around(sent.reshape(owners, CAP, width), "z").reshape(rows, width)
    held, whole, weights, got = lax.optimization_barrier((held, whole, weights, got))
    late = assemble(0, *weights, got)
    held, whole, late = lax.optimization_barrier((held, whole, late))
    full = around(jnp.broadcast_to(held[None], (chips, rows, width)), "x")
    out = call(ffn_kernel, shape(BF16, chips, rows, width), index, full, late, whole, limit=12 << 20)
    terms = around(out, "x")
    summed = jnp.sum(terms.astype(F32), axis=0).astype(BF16)
    back = around(summed.reshape(owners, CAP, width), "z").reshape(rows, width)
    mine = call(combine_kernel, shape(BF16, tokens, width), weight, back)
    both = call(merge_kernel, shape(BF16, chips, tokens, width), mine, swap(mine))
    return call(output_kernel, shape(BF16, tokens, up_proj.shape[1]), around(both, "x"), up_proj)


def solution(mesh):
    shape = mesh.devices.shape
    split = Mesh(mesh.devices.reshape(shape[0], shape[1], shape[2] // 2, 2), ("dp", "z", "x", "c"))
    tensor = ("x", "c")
    in_specs = (
        P(("dp", "z"), tensor),
        P(("dp", "z"), None),
        P(("dp", "z"), None),
        P(tensor, None),
        P("z", None, tensor),
        P("z", None, tensor),
        P("z", tensor, None),
        P(None, tensor),
    )
    return jax.shard_map(body, mesh=split, in_specs=in_specs, out_specs=P(("dp", "z"), tensor), check_vma=False)
```
